256 devices in a mesh: orb: 4 (over z_hi), grid: 64 (over y, x, z_lo, core).
Axes of the slice: x: 4, y: 4, z: 8 (z_hi: 4, z_lo: 2; z = z_hi * 2 + z_lo), core: 2. Of those that a mesh axis runs over, the one named last changes fastest.
Arguments:
- orbitals: bfloat16 [512, 884736], P(('orb', 'grid')), may hold values from -6 to 6
- potential: float32 [884736], replicated, may hold values from -1 to 1
- subspace: bfloat16 [512, 512], P(('orb', 'grid')), may hold values from -0.25 to 0.25
Outputs:
- rotated: bfloat16 [512, 884736], P(None, ('orb', 'grid'))
The draws below stay inside these ranges and needn't reach their ends.
All inputs are finite; a program needn't handle non-finite values.
Results may differ from the reference program's by a relative error of at most 0.0049.
Values may be sent and summed in bfloat16 or wider, within the bound.
A program may use at most 128 MiB of HBM per device.

```python
import jax
import jax.numpy as jnp
from jax import lax

GRID_N = 96
DEG = 6
NORB = 512
NCELL = 884736


def levels(rng, dims, shards, smallest, largest):
    factor_of, own = 1.0, jax.random.fold_in(rng, 6)
    for axis_at, parts in shards:
        heights = jnp.exp(jax.random.uniform(jax.random.fold_in(own, axis_at), (parts,), jnp.float32, smallest / len(shards), largest / len(shards)))
        factor_of = factor_of * jnp.repeat(heights, dims[axis_at] // parts).reshape([-1 if axis == axis_at else 1 for axis in range(len(dims))])
    return factor_of


def scatter_about(rng, dims, scale, limit, split=(), dtype=jnp.bfloat16):
    entries = scale * jax.random.normal(rng, dims, jnp.float32)
    if split:
        entries = entries * levels(rng, dims, split, -0.22, 0.18)
    return jnp.clip(entries, -limit, limit).astype(dtype)


def setup_inputs(seed: int = 0) -> dict:
    key_list = jax.random.split(jax.random.key(seed), 4)
    return {
        "orbitals": scatter_about(key_list[0], (NORB, NCELL), 1.0, 6.0, ((0, 256),)),
        "potential": jnp.clip(jax.random.uniform(key_list[1], (NCELL,), jnp.float32, -1.0, 1.0), -1.0, 1.0),
        "subspace": scatter_about(key_list[2], (NORB, NORB), NORB ** -0.5, 0.25, ((0, 256),)),
    }


top_bound = 12.0
cut_bound = 0.0
low_bound = -0.25


def pair_sum(values, axis):
    widths = [(0, 0), (0, 0), (0, 0), (0, 0)]
    widths[axis] = (1, 1)
    padded = jnp.pad(values, widths)
    length = values.shape[axis]
    return lax.slice_in_dim(padded, 2, length + 2, axis=axis) + lax.slice_in_dim(padded, 0, length, axis=axis)


def hamiltonian(values, shaped_pot):
    rows_sum = pair_sum(values, 1)
    cols_sum = pair_sum(values, 2)
    depth_sum = pair_sum(values, 3)
    faces = rows_sum + cols_sum + depth_sum
    edges = pair_sum(cols_sum + depth_sum, 1) + pair_sum(depth_sum, 2)
    return (8.0 + shaped_pot) * values - (2.0 / 3.0) * faces - (1.0 / 3.0) * edges


def chebyshev_filter(block, shaped_pot):
    half_width = (top_bound - cut_bound) / 2.0
    centre = (top_bound + cut_bound) / 2.0
    sigma_old = half_width / (low_bound - centre)
    ratio_inverse = 2.0 / sigma_old
    older = block.astype(jnp.float32)
    current = (hamiltonian(older, shaped_pot) - centre * older) * (sigma_old / half_width)
    for order_index in range(2, DEG + 1):
        sigma_new = 1.0 / (ratio_inverse - sigma_old)
        newer = (hamiltonian(current, shaped_pot) - centre * current) * (2.0 * sigma_new / half_width) - (sigma_old * sigma_new) * older
        older = current
        current = newer
        sigma_old = sigma_new
    return current


def reference(orbitals, potential, subspace):
    shaped_pot = potential.reshape(1, GRID_N, GRID_N, GRID_N)
    shaped = orbitals.reshape(NORB // 8, 8, GRID_N, GRID_N, GRID_N)
    filtered = lax.map(lambda block: chebyshev_filter(block, shaped_pot).astype(jnp.bfloat16), shaped)
    plane_cells = GRID_N * GRID_N
    column_blocks = filtered.reshape(NORB, GRID_N, plane_cells).transpose(1, 0, 2)
    matrix = subspace.T.astype(jnp.float32)

    def rotate(columns):
        return jnp.dot(matrix, columns.astype(jnp.float32), preferred_element_type=jnp.float32).astype(jnp.bfloat16)

    rotated = lax.map(rotate, column_blocks)
    return rotated.transpose(1, 0, 2).reshape(NORB, NCELL)
```

```python
import jax
import jax.numpy as jnp
from jax import lax
from jax.experimental import pallas as pl
from jax.experimental.pallas import tpu as pltpu
from jax.sharding import PartitionSpec as P

GRID_N = 96
DEG = 6


top_bound = 12.0
cut_bound = 0.0
low_bound = -0.25


def along_rows(values):
    length = values.shape[1]
    padded = jnp.pad(values, ((0, 0), (1, 1), (0, 0)))
    return padded[:, 2 : length + 2, :] + padded[:, 0:length, :]


def along_columns(values, grid_side):
    width = values.shape[2]
    padded = jnp.pad(values, ((0, 0), (0, 0), (grid_side, grid_side)))
    return padded[:, :, 2 * grid_side : width + 2 * grid_side] + padded[:, :, 0:width]


def along_depth(values, upper_mask, lower_mask):
    width = values.shape[2]
    padded = jnp.pad(values, ((0, 0), (0, 0), (1, 1)))
    return padded[:, :, 2 : width + 2] * upper_mask + padded[:, :, 0:width] * lower_mask


def hamiltonian(values, shaped_pot, upper_mask, lower_mask):
    rows_sum = along_rows(values)
    cols_sum = along_columns(values, GRID_N)
    depth_sum = along_depth(values, upper_mask, lower_mask)
    faces = rows_sum + cols_sum + depth_sum
    edges = along_rows(cols_sum + depth_sum) + along_columns(depth_sum, GRID_N)
    return (8.0 + shaped_pot) * values - 2.0 / 3.0 * faces - 1.0 / 3.0 * edges


def chebyshev_filter(fields, shaped_pot, upper_mask, lower_mask):
    half_width = (top_bound - cut_bound) / 2.0
    centre = (top_bound + cut_bound) / 2.0
    sigma_old = half_width / (low_bound - centre)
    ratio_inverse = 2.0 / sigma_old
    first_scale = sigma_old / half_width
    step_scales = []
    old_scales = []
    for order_index in range(2, DEG + 1):
        sigma_new = 1.0 / (ratio_inverse - sigma_old)
        step_scales.append(2.0 * sigma_new / half_width)
        old_scales.append(sigma_old * sigma_new)
        sigma_old = sigma_new
    step_table = jnp.array(step_scales, dtype=jnp.float32)
    old_table = jnp.array(old_scales, dtype=jnp.float32)
    current = (
        hamiltonian(fields, shaped_pot, upper_mask, lower_mask) - centre * fields
    ) * first_scale

    def advance(order_index, carried):
        older, present = carried
        applied = hamiltonian(present, shaped_pot, upper_mask, lower_mask)
        newer = (applied - centre * present) * step_table[order_index] - old_table[
            order_index
        ] * older
        return (present, newer)

    older, current = lax.fori_loop(0, DEG - 1, advance, (fields, current))
    return current


DEVICES = 256
BLOCKS = 27
MESH = pl.DeviceIdType.MESH


def torus_peer(orb, grid, step):
    mixed = lax.rem(step * 91, DEVICES)
    z = orb * 2 + lax.rem(grid // 2, 2)
    z = lax.rem(z + mixed // 32, 8)
    y = lax.rem(grid // 16 + lax.rem(mixed // 8, 4), 4)
    x = lax.rem(lax.rem(grid // 4, 4) + lax.rem(mixed // 2, 4), 4)
    core = lax.rem(grid + lax.rem(mixed, 2), 2)
    return z // 2, y * 16 + x * 4 + lax.rem(z, 2) * 2 + core


def exchange_kernel(source, landed, send_sem, recv_sem):
    orb, grid = lax.axis_index("orb"), lax.axis_index("grid")
    me = orb * 64 + grid
    barrier = pltpu.get_barrier_semaphore()

    def greet(step, carry):
        peer_orb, peer_grid = torus_peer(orb, grid, step)
        pl.semaphore_signal(barrier, inc=1, device_id=(peer_orb, peer_grid), device_id_type=MESH)
        return carry

    lax.fori_loop(1, DEVICES, greet, 0)
    pl.semaphore_wait(barrier, DEVICES - 1)

    def send(step, carry):
        peer_orb, peer_grid = torus_peer(orb, grid, step)
        pltpu.make_async_remote_copy(
            source.at[peer_orb * 64 + peer_grid], landed.at[:, me], send_sem, recv_sem,
            device_id=(peer_orb, peer_grid), device_id_type=MESH,
        ).start()
        return carry

    lax.fori_loop(1, DEVICES, send, 0)
    pltpu.make_async_copy(source.at[me], landed.at[:, me], recv_sem).start()
    pltpu.make_async_copy(landed, landed, recv_sem).wait()
    sent = source.at[pl.ds(0, DEVICES - 1)]
    pltpu.make_async_copy(sent, sent, send_sem).wait()


def exchange(source):
    return pl.pallas_call(
        exchange_kernel,
        out_shape=jax.ShapeDtypeStruct((BLOCKS, DEVICES, 2, 128), jnp.bfloat16),
        in_specs=[pl.BlockSpec(memory_space=pltpu.VMEM)],
        out_specs=pl.BlockSpec(memory_space=pltpu.VMEM),
        scratch_shapes=[pltpu.SemaphoreType.DMA, pltpu.SemaphoreType.DMA],
        compiler_params=pltpu.CompilerParams(
            collective_id=0, has_side_effects=True, vmem_limit_bytes=32 * 2**20
        ),
        name="exchange",
    )(source)


def rotate_kernel(matrix, fields, rotated):
    wide = jnp.concatenate([fields[i] for i in range(3)], axis=1)
    rotated[...] = lax.dot_general(
        matrix[...], wide, (((0,), (0,)), ((), ())), preferred_element_type=jnp.float32
    ).astype(jnp.bfloat16)


def rotate(matrix, fields):
    return pl.pallas_call(
        rotate_kernel,
        grid=(BLOCKS // 3,),
        out_shape=jax.ShapeDtypeStruct((512, BLOCKS * 128), jnp.bfloat16),
        in_specs=[
            pl.BlockSpec((512, 512), lambda i: (0, 0)),
            pl.BlockSpec((3, 512, 128), lambda i: (i, 0, 0)),
        ],
        out_specs=pl.BlockSpec((512, 384), lambda i: (0, i)),
        compiler_params=pltpu.CompilerParams(vmem_limit_bytes=32 * 2**20),
        name="rotate",
    )(matrix, fields)


def local(orbitals, potential, subspace):
    local_count = orbitals.shape[0]
    grid_side = GRID_N
    plane = grid_side * grid_side
    fields = orbitals.astype(jnp.float32).reshape(local_count, grid_side, plane)
    shaped_pot = potential.reshape(1, grid_side, plane)
    depth_index = jnp.arange(plane, dtype=jnp.int32) % grid_side
    upper_mask = (depth_index < grid_side - 1).astype(jnp.float32)
    lower_mask = (depth_index > 0).astype(jnp.float32)
    result = chebyshev_filter(fields, shaped_pot, upper_mask, lower_mask)
    filtered = result.astype(jnp.bfloat16).reshape(local_count, DEVICES, BLOCKS, 128)
    matrix = lax.all_gather(subspace, ("orb", "grid"), axis=0, tiled=True)
    landed = exchange(filtered.transpose(1, 2, 0, 3))
    return rotate(matrix, landed.reshape(BLOCKS, 512, 128))


def solution(mesh):
    placed = (P(("orb", "grid"), None), P(), P(("orb", "grid"), None))
    return jax.shard_map(
        local, mesh=mesh, in_specs=placed, out_specs=P(None, ("orb", "grid")), check_vma=False
    )
```

```python
import jax
import jax.numpy as jnp
from jax import lax
from jax.experimental import pallas as pl
from jax.experimental.pallas import tpu as pltpu
from jax.sharding import PartitionSpec as P

SIDE = 96
DEG = 6
DEVICES = 256
BLOCKS = 27
FLAT = 72
PERIOD = SIDE + 1
STEPS = PERIOD + 2 * DEG
MESH = pl.DeviceIdType.MESH

TOP = 12.0
CUT = 0.0
LOW = -0.25
HALF = (TOP - CUT) / 2.0
CENTRE = (TOP + CUT) / 2.0


def last_scale():
    at = (LOW - CENTRE) / HALF
    older, current = 1.0, at
    for _ in range(DEG - 1):
        older, current = current, 2.0 * at * current - older
    return 1.0 / current


def torus_peer(orb, grid, step):
    z = orb * 2 + lax.rem(grid // 2, 2)
    z = lax.rem(z + step // 32, 8)
    y = lax.rem(grid // 16 + lax.rem(step // 8, 4), 4)
    x = lax.rem(lax.rem(grid // 4, 4) + lax.rem(step // 2, 4), 4)
    core = lax.rem(grid + lax.rem(step, 2), 2)
    return z // 2, y * 16 + x * 4 + lax.rem(z, 2) * 2 + core


def sweep_kernel(
    orbitals, potential, subspace, landed, matrix,
    ring, wells, raw, packed, staged,
    send_sem, recv_sem, near_send, near_recv, far_send, far_recv,
):
    orb, grid = lax.axis_index("orb"), lax.axis_index("grid")
    me = orb * 64 + grid
    column = grid // 4 * 2 + lax.rem(grid, 2)
    depth = orb * 2 + lax.rem(grid // 2, 2)
    slot_of_me = column * 8 + depth
    downward = lax.rem(grid, 2)
    barrier = pltpu.get_barrier_semaphore()

    def greet(step, carry):
        peer = torus_peer(orb, grid, step)
        pl.semaphore_signal(barrier, inc=1, device_id=peer, device_id_type=MESH)
        return carry

    lax.fori_loop(1, DEVICES, greet, 0)

    lane = lax.broadcasted_iota(jnp.int32, (8, 128), 1)
    inside = lane < SIDE
    ones = jnp.where(inside, 1.0, 0.0).astype(jnp.float32)
    zeros = jnp.zeros((8, 128), jnp.float32)

    def clear(at, carry):
        for own in range(2):
            for group in range(4):
                ring[at // 4, lax.rem(at, 4), own, group, pl.ds(0, 8), :] = zeros
                ring[at // 4, lax.rem(at, 4), own, group, pl.ds(32, 8), :] = zeros
        return carry

    lax.fori_loop(0, DEG * 4, clear, 0)

    own_plane = me * 3 // 8 // 3 * 3
    ordered = jnp.where(downward == 1, SIDE - 3 - own_plane, own_plane)
    base = lax.rem(ordered + 24, SIDE) - DEG + PERIOD

    def position(number):
        return lax.rem(base + number, PERIOD)

    def plane_of(place):
        return jnp.where(downward == 1, SIDE - 1 - place, place)

    def to_lines(rows):
        first, second, third = rows
        return (
            jnp.where(inside, first, 0.0),
            jnp.where(inside, pltpu.roll(jnp.where(lane >= 96, first, second), 32, 1), 0.0),
            jnp.where(inside, pltpu.roll(jnp.where(lane >= 64, second, third), 64, 1), 0.0),
            jnp.where(inside, pltpu.roll(third, 96, 1), 0.0),
        )

    def to_rows(lines):
        early = pltpu.roll(lines[1], 96, 1)
        middle = pltpu.roll(lines[2], 64, 1)
        late = pltpu.roll(lines[3], 32, 1)
        return (
            jnp.where(lane < 96, lines[0], early),
            jnp.where(lane < 64, early, middle),
            jnp.where(lane < 32, middle, late),
        )

    def zero_plane(stage, slot):
        for own in range(2):
            for group in range(4):
                for part in range(3):
                    ring[stage, slot, own, group, pl.ds(8 + 8 * part, 8), :] = zeros

    def take(time):
        place = position(time)
        slot = lax.rem(time, 4)
        well = lax.rem(time, 8)

        @pl.when(place < SIDE)
        def _():
            plane = plane_of(place)
            raw[...] = orbitals[plane].astype(jnp.float32)
            for part in range(3):
                rows = [potential[plane, pl.ds(24 * part + j, 8, stride=3), :] for j in range(3)]
                for group, line in enumerate(to_lines(rows)):
                    wells[well, group, pl.ds(8 * part, 8), :] = 3.0 * line + 6.0
                for own in range(2):
                    rows = [raw[pl.ds(48 * part + 2 * j + own, 8, stride=6), :] for j in range(3)]
                    for group, line in enumerate(to_lines(rows)):
                        ring[0, slot, own, group, pl.ds(8 + 8 * part, 8), :] = line

        @pl.when(place == SIDE)
        def _():
            zero_plane(0, slot)

    def advance(stage, number, own, part):
        def read(plane):
            at = lax.rem(plane + 4, 4)
            rows = [
                ring[stage - 1, at, own, group, pl.ds(8 + 8 * part, 8), :] for group in range(4)
            ]
            before = ring[stage - 1, at, own, 3, pl.ds(7 + 8 * part, 8), :]
            after = ring[stage - 1, at, own, 0, pl.ds(9 + 8 * part, 8), :]
            return [before] + rows + [after]

        behind, here, ahead = read(number - 1), read(number), read(number + 1)
        across = [u + v for u, v in zip(behind, ahead)]
        if stage == 1:
            factor = 0.5 * ones
        elif stage == DEG:
            factor = (last_scale() / 81.0) * ones
        elif stage % 2:
            factor = ones
        else:
            factor = (1.0 / 81.0) * ones
        made = []
        for group in range(4):
            centre = here[group + 1]
            both = across[group + 1] + (here[group] + here[group + 2])
            wide = both + (centre + centre)
            along = pltpu.roll(wide, 1, 1) + pltpu.roll(wide, 127, 1)
            total = (both + both) + (across[group] + across[group + 2]) + along
            well = wells[lax.rem(number + 8, 8), group, pl.ds(8 * part, 8), :]
            value = (total - well * centre) * factor
            if stage > 1:
                older = ring[
                    stage - 2, lax.rem(number + 4, 4), own, group, pl.ds(8 + 8 * part, 8), :
                ]
                value = value - (older * last_scale() if stage == DEG else older)
            made.append(value)
        return made

    def middle_stage(stage, time):
        number = time - stage
        place = position(number)
        slot = lax.rem(number + 8, 4)
        active = time >= 2 * stage

        @pl.when(jnp.logical_and(active, place < SIDE))
        def _():
            for own in range(2):
                for part in range(3):
                    for group, value in enumerate(advance(stage, number, own, part)):
                        ring[stage, slot, own, group, pl.ds(8 + 8 * part, 8), :] = value

        @pl.when(jnp.logical_and(active, place == SIDE))
        def _():
            zero_plane(stage, slot)

    def last_stage(time):
        number = time - DEG
        place = position(number)

        @pl.when(jnp.logical_and(time >= 2 * DEG, place < SIDE))
        def _():
            plane = plane_of(place)
            for own in range(2):
                for part in range(3):
                    rows = to_rows(advance(DEG, number, own, part))
                    for j in range(3):
                        packed[pl.ds(48 * part + 2 * j + own, 8, stride=6), :] = rows[j]
            pairs = packed[...].astype(jnp.bfloat16).reshape(FLAT, 2, 128)
            staged[pl.ds(FLAT * plane, FLAT)] = pairs
            upward = 1 - downward
            low = (8 * plane + 2 * downward) // 3
            high = (8 * (plane + 1) + 2 * (1 - upward)) // 3

            def send(target, carry):
                @pl.when(target == me)
                def _():
                    pltpu.make_async_copy(
                        staged.at[pl.ds(BLOCKS * target, BLOCKS)], landed.at[:, slot_of_me], recv_sem
                    ).start()

                @pl.when(target != me)
                def _():
                    pltpu.make_async_remote_copy(
                        staged.at[pl.ds(BLOCKS * target, BLOCKS)], landed.at[:, slot_of_me],
                        send_sem, recv_sem,
                        device_id=(target // 64, lax.rem(target, 64)), device_id_type=MESH,
                    ).start()

                return carry

            lax.fori_loop(low, high, send, 0)

    def step(time, carry):
        @pl.when(time == 2 * DEG - 1)
        def _():
            pl.semaphore_wait(barrier, DEVICES - 1)
            pltpu.make_async_copy(subspace, matrix.at[:, column, depth], near_recv).start()

            def send(offset, inner):
                peer = torus_peer(orb, grid, offset * 32)
                pltpu.make_async_remote_copy(
                    subspace, matrix.at[:, column, depth], near_send, near_recv,
                    device_id=peer, device_id_type=MESH,
                ).start()
                return inner

            lax.fori_loop(1, 8, send, 0)

        @pl.when(time == 40)
        def _():
            group = matrix.at[:, column]
            pltpu.make_async_copy(group, group, near_recv).wait()

            def send(offset, inner):
                peer = torus_peer(orb, grid, offset)
                pltpu.make_async_remote_copy(
                    matrix.at[:, column], matrix.at[:, column], far_send, far_recv,
                    device_id=peer, device_id_type=MESH,
                ).start()
                return inner

            lax.fori_loop(1, 32, send, 0)

        take(time)
        for stage in range(1, DEG):
            middle_stage(stage, time)
        last_stage(time)
        return carry

    lax.fori_loop(0, STEPS, step, 0)

    near = matrix.at[:, 0, pl.ds(0, 7)]
    pltpu.make_async_copy(near, near, near_send).wait()
    far = matrix.at[:, pl.ds(0, 31)]
    pltpu.make_async_copy(far, far, far_recv).wait()
    pltpu.make_async_copy(far, far, far_send).wait()
    pltpu.make_async_copy(landed, landed, recv_sem).wait()
    sent = staged.at[pl.ds(0, BLOCKS * (DEVICES - 1))]
    pltpu.make_async_copy(sent, sent, send_sem).wait()


def sweep(orbitals, potential, subspace):
    vmem = pl.BlockSpec(memory_space=pltpu.VMEM)
    return pl.pallas_call(
        sweep_kernel,
        out_shape=(
            jax.ShapeDtypeStruct((BLOCKS, DEVICES, 2, 128), jnp.bfloat16),
            jax.ShapeDtypeStruct((4, 32, 8, 2, 128), jnp.bfloat16),
        ),
        in_specs=[vmem, vmem, vmem],
        out_specs=(vmem, vmem),
        scratch_shapes=[
            pltpu.VMEM((DEG, 4, 2, 4, 40, 128), jnp.float32),
            pltpu.VMEM((8, 4, 24, 128), jnp.float32),
            pltpu.VMEM((2 * FLAT, 128), jnp.float32),
            pltpu.VMEM((2 * FLAT, 128), jnp.float32),
            pltpu.VMEM((SIDE * FLAT, 2, 128), jnp.bfloat16),
        ] + [pltpu.SemaphoreType.DMA] * 6,
        compiler_params=pltpu.CompilerParams(
            collective_id=0, has_side_effects=True, vmem_limit_bytes=40 * 2**20
        ),
        name="sweep",
    )(orbitals, potential, subspace)


def rotate_kernel(matrix, fields, rotated):
    mixing = jnp.concatenate([matrix[i] for i in range(4)], axis=1)
    wide = jnp.concatenate([fields[i] for i in range(3)], axis=1)
    rotated[...] = lax.dot_general(
        mixing, wide, (((0,), (0,)), ((), ())), preferred_element_type=jnp.float32
    ).astype(jnp.bfloat16)


def rotate(matrix, fields):
    return pl.pallas_call(
        rotate_kernel,
        grid=(BLOCKS // 3,),
        out_shape=jax.ShapeDtypeStruct((512, BLOCKS * 128), jnp.bfloat16),
        in_specs=[
            pl.BlockSpec((4, 512, 128), lambda i: (0, 0, 0)),
            pl.BlockSpec((3, 512, 128), lambda i: (i, 0, 0)),
        ],
        out_specs=pl.BlockSpec((512, 384), lambda i: (0, i)),
        compiler_params=pltpu.CompilerParams(vmem_limit_bytes=32 * 2**20),
        name="rotate",
    )(matrix, fields)


def local(orbitals, potential, subspace):
    pairs = orbitals.reshape(2, SIDE * FLAT, 128).transpose(1, 0, 2)
    fields, matrix = sweep(
        pairs.reshape(SIDE, 2 * FLAT, 128),
        potential.reshape(SIDE, FLAT, 128),
        subspace.reshape(2, 4, 128).transpose(1, 0, 2),
    )
    return rotate(matrix.reshape(4, 512, 128), fields.reshape(BLOCKS, 512, 128))


def solution(mesh):
    placed = (P(("orb", "grid"), None), P(), P(("orb", "grid"), None))
    return jax.shard_map(
        local, mesh=mesh, in_specs=placed, out_specs=P(None, ("orb", "grid")), check_vma=False
    )
```

```python
import functools

import jax
import jax.numpy as jnp
from jax import lax
from jax.experimental import pallas as pl
from jax.experimental.pallas import tpu as pltpu
from jax.sharding import PartitionSpec as P

SIDE = 96
DEG = 6
DEVICES = 256
BLOCKS = 27
FLAT = 72
PERIOD = SIDE + 1
STEPS = PERIOD + 3 * DEG + 1
READY = 3 * DEG + 1
GROUPS = 4
MESH = pl.DeviceIdType.MESH

TOP = 12.0
CUT = 0.0
LOW = -0.25
HALF = (TOP - CUT) / 2.0
CENTRE = (TOP + CUT) / 2.0


def last_scale():
    at = (LOW - CENTRE) / HALF
    older, current = 1.0, at
    for _ in range(DEG - 1):
        older, current = current, 2.0 * at * current - older
    return 1.0 / current


def torus_peer(orb, grid, step):
    z = orb * 2 + lax.rem(grid // 2, 2)
    z = lax.rem(z + step // 32, 8)
    y = lax.rem(grid // 16 + lax.rem(step // 8, 4), 4)
    x = lax.rem(lax.rem(grid // 4, 4) + lax.rem(step // 2, 4), 4)
    core = lax.rem(grid + lax.rem(step, 2), 2)
    return z // 2, y * 16 + x * 4 + lax.rem(z, 2) * 2 + core


def sweep_kernel(
    orbitals_hbm, potential_hbm, subspace, landed, matrix,
    orbitals, potential, ring0, ring1, ring2, ring3, ring4, ring5, wells, raw, packed, staged,
    send_sem, recv_sem, near_send, near_recv, far_send, far_recv, orbitals_sem, potential_sem,
):
    ring = (ring0, ring1, ring2, ring3, ring4, ring5)
    orb, grid = lax.axis_index("orb"), lax.axis_index("grid")
    me = orb * 64 + grid
    column = grid // 4 * 2 + lax.rem(grid, 2)
    depth = orb * 2 + lax.rem(grid // 2, 2)
    slot_of_me = column * 8 + depth
    downward = lax.rem(grid, 2)
    barrier = pltpu.get_barrier_semaphore()
    fetches = (
        pltpu.make_async_copy(orbitals_hbm, orbitals, orbitals_sem),
        pltpu.make_async_copy(potential_hbm, potential, potential_sem),
    )
    for fetch in fetches:
        fetch.start()

    def greet(step, carry):
        peer = torus_peer(orb, grid, step)
        pl.semaphore_signal(barrier, inc=1, device_id=peer, device_id_type=MESH)
        return carry

    lax.fori_loop(1, DEVICES, greet, 0)

    lane = lax.broadcasted_iota(jnp.int32, (8, 128), 1)
    inside = lane < SIDE
    ones = jnp.where(inside, 1.0, 0.0).astype(jnp.float32)
    zeros = jnp.zeros((8, 128), jnp.float32)

    def clear(at, carry):
        for held in ring:
            for own in range(2):
                for group in range(GROUPS):
                    held[at, own, group, pl.ds(0, 8), :] = zeros
                    held[at, own, group, pl.ds(32, 8), :] = zeros
        return carry

    lax.fori_loop(0, 4, clear, 0)
    for fetch in fetches:
        fetch.wait()

    own_plane = me * 3 // 8 // 3 * 3
    ordered = jnp.where(downward == 1, SIDE - 3 - own_plane, own_plane)
    base = lax.rem(ordered + 24, SIDE) - DEG + PERIOD

    def position(number):
        return lax.rem(base + number, PERIOD)

    def plane_of(place):
        return jnp.where(downward == 1, SIDE - 1 - place, place)

    def to_lines(rows):
        first, second, third = rows
        return (
            jnp.where(inside, first, 0.0),
            jnp.where(inside, pltpu.roll(jnp.where(lane >= 96, first, second), 32, 1), 0.0),
            jnp.where(inside, pltpu.roll(jnp.where(lane >= 64, second, third), 64, 1), 0.0),
            jnp.where(inside, pltpu.roll(third, 96, 1), 0.0),
        )

    def to_rows(lines):
        early = pltpu.roll(lines[1], 96, 1)
        middle = pltpu.roll(lines[2], 64, 1)
        late = pltpu.roll(lines[3], 32, 1)
        return (
            jnp.where(lane < 96, lines[0], early),
            jnp.where(lane < 64, early, middle),
            jnp.where(lane < 32, middle, late),
        )

    def keep(stage, slot, own, part, values):
        rows = pl.ds(8 + 8 * part, 8)
        for group, value in enumerate(values):
            ring[stage][slot, own, group, rows, :] = value

    def zero_plane(stage, number):
        slot = lax.rem(number + 64, 4)
        place = position(number)

        @pl.when(place == SIDE)
        def _():
            for own in range(2):
                for part in range(3):
                    keep(stage, slot, own, part, [zeros] * 4)

    def take(time):
        place = position(time)
        slot = lax.rem(time, 4)
        well = lax.rem(time, 16)
        plane = plane_of(jnp.minimum(place, SIDE - 1))
        raw[...] = orbitals[plane].astype(jnp.float32)
        for part in range(3):
            rows = [potential[plane, pl.ds(24 * part + j, 8, stride=3), :] for j in range(3)]
            for group, line in enumerate(to_lines(rows)):
                wells[well, group, pl.ds(8 * part, 8), :] = 3.0 * line + 6.0
            for own in range(2):
                rows = [raw[pl.ds(48 * part + 2 * j + own, 8, stride=6), :] for j in range(3)]
                keep(0, slot, own, part, to_lines(rows))

    def advance(stage, number, own, part):
        def read(plane):
            at = lax.rem(plane + 64, 4)
            rows = [
                ring[stage - 1][at, own, group, pl.ds(8 + 8 * part, 8), :] for group in range(4)
            ]
            before = ring[stage - 1][at, own, 3, pl.ds(7 + 8 * part, 8), :]
            after = ring[stage - 1][at, own, 0, pl.ds(9 + 8 * part, 8), :]
            return [before] + rows + [after]

        behind, here, ahead = read(number - 1), read(number), read(number + 1)
        across = [u + v for u, v in zip(behind, ahead)]
        if stage == 1:
            factor = 0.5 * ones
        elif stage == DEG:
            factor = (last_scale() / 81.0) * ones
        elif stage % 2:
            factor = ones
        else:
            factor = (1.0 / 81.0) * ones
        made = []
        for group in range(4):
            centre = here[group + 1]
            both = across[group + 1] + (here[group] + here[group + 2])
            wide = both + (centre + centre)
            along = pltpu.roll(wide, 1, 1) + pltpu.roll(wide, 127, 1)
            total = (both + both) + (across[group] + across[group + 2]) + along
            well = wells[lax.rem(number + 64, 16), group, pl.ds(8 * part, 8), :]
            value = (total - well * centre) * factor
            if stage > 1:
                older = ring[stage - 2][
                    lax.rem(number + 64, 4), own, group, pl.ds(8 + 8 * part, 8), :
                ]
                value = value - (older * last_scale() if stage == DEG else older)
            made.append(value)
        return made

    def pack(time):
        place = position(time - 2 * DEG - 1)

        @pl.when(jnp.logical_and(time >= READY, place < SIDE))
        def _():
            plane = plane_of(place)
            pairs = packed[...].astype(jnp.bfloat16).reshape(FLAT, 2, 128)
            staged[pl.ds(FLAT * plane, FLAT)] = pairs
            low = (8 * plane + 2 * downward) // 3
            high = (8 * (plane + 1) + 2 * downward) // 3

            def send(target, carry):
                @pl.when(target == me)
                def _():
                    pltpu.make_async_copy(
                        staged.at[pl.ds(BLOCKS * target, BLOCKS)], landed.at[:, slot_of_me], recv_sem
                    ).start()

                @pl.when(target != me)
                def _():
                    pltpu.make_async_remote_copy(
                        staged.at[pl.ds(BLOCKS * target, BLOCKS)], landed.at[:, slot_of_me],
                        send_sem, recv_sem,
                        device_id=(target // 64, lax.rem(target, 64)), device_id_type=MESH,
                    ).start()

                return carry

            lax.fori_loop(low, high, send, 0)

    def stages(deepest, time):
        for stage in range(deepest, 0, -1):
            number = time - 2 * stage
            slot = lax.rem(number + 64, 4)
            for own in range(2):
                for part in range(3):
                    keep(stage, slot, own, part, advance(stage, number, own, part))
        take(time)
        for stage in range(deepest + 1):
            zero_plane(stage, time - 2 * stage)

    def warm(deepest, time, carry):
        stages(deepest, time)
        return carry

    def step(time, carry):
        @pl.when(time == READY - 1)
        def _():
            pl.semaphore_wait(barrier, DEVICES - 1)
            pltpu.make_async_copy(subspace, matrix.at[:, column, depth], near_recv).start()

            def send(offset, inner):
                peer = torus_peer(orb, grid, offset * 32)
                pltpu.make_async_remote_copy(
                    subspace, matrix.at[:, column, depth], near_send, near_recv,
                    device_id=peer, device_id_type=MESH,
                ).start()
                return inner

            lax.fori_loop(1, 8, send, 0)

        @pl.when(time == 50)
        def _():
            group = matrix.at[:, column]
            pltpu.make_async_copy(group, group, near_recv).wait()

            def send(offset, inner):
                peer = torus_peer(orb, grid, offset)
                pltpu.make_async_remote_copy(
                    matrix.at[:, column], matrix.at[:, column], far_send, far_recv,
                    device_id=peer, device_id_type=MESH,
                ).start()
                return inner

            lax.fori_loop(1, 32, send, 0)

        pack(time)
        for own in range(2):
            for part in range(3):
                rows = to_rows(advance(DEG, time - 2 * DEG, own, part))
                for j in range(3):
                    packed[pl.ds(48 * part + 2 * j + own, 8, stride=6), :] = rows[j]
        stages(DEG - 1, time)
        return carry

    for deepest in (1, 3, 5):
        start = 3 * deepest - 3
        lax.fori_loop(start, start + 6, functools.partial(warm, deepest), 0)
    lax.fori_loop(3 * DEG, STEPS, step, 0)

    near = matrix.at[:, 0, pl.ds(0, 7)]
    pltpu.make_async_copy(near, near, near_send).wait()
    far = matrix.at[:, pl.ds(0, 31)]
    pltpu.make_async_copy(far, far, far_recv).wait()
    pltpu.make_async_copy(far, far, far_send).wait()
    pltpu.make_async_copy(landed, landed, recv_sem).wait()
    sent = staged.at[pl.ds(0, BLOCKS * (DEVICES - 1))]
    pltpu.make_async_copy(sent, sent, send_sem).wait()


def sweep(orbitals, potential, subspace):
    vmem = pl.BlockSpec(memory_space=pltpu.VMEM)
    hbm = pl.BlockSpec(memory_space=pltpu.HBM)
    return pl.pallas_call(
        sweep_kernel,
        out_shape=(
            jax.ShapeDtypeStruct((BLOCKS, DEVICES, 2, 128), jnp.bfloat16),
            jax.ShapeDtypeStruct((4, 32, 8, 2, 128), jnp.bfloat16),
        ),
        in_specs=[hbm, hbm, vmem],
        out_specs=(vmem, vmem),
        scratch_shapes=[
            pltpu.VMEM((SIDE, 2 * FLAT, 128), jnp.bfloat16),
            pltpu.VMEM((SIDE, FLAT, 128), jnp.float32),
        ] + [pltpu.VMEM((4, 2, GROUPS, 40, 128), jnp.float32)] * DEG + [
            pltpu.VMEM((16, 4, 24, 128), jnp.float32),
            pltpu.VMEM((2 * FLAT, 128), jnp.float32),
            pltpu.VMEM((2 * FLAT, 128), jnp.float32),
            pltpu.VMEM((SIDE * FLAT, 2, 128), jnp.bfloat16),
        ] + [pltpu.SemaphoreType.DMA] * 8,
        compiler_params=pltpu.CompilerParams(
            collective_id=0, has_side_effects=True, vmem_limit_bytes=40 * 2**20
        ),
        name="sweep",
    )(orbitals, potential, subspace)


def rotate_kernel(matrix, fields, rotated):
    mixing = jnp.concatenate([matrix[i] for i in range(4)], axis=1)
    wide = jnp.concatenate([fields[i] for i in range(3)], axis=1)
    rotated[...] = lax.dot_general(
        mixing, wide, (((0,), (0,)), ((), ())), preferred_element_type=jnp.float32
    ).astype(jnp.bfloat16)


def rotate(matrix, fields):
    return pl.pallas_call(
        rotate_kernel,
        grid=(BLOCKS // 3,),
        out_shape=jax.ShapeDtypeStruct((512, BLOCKS * 128), jnp.bfloat16),
        in_specs=[
            pl.BlockSpec((4, 512, 128), lambda i: (0, 0, 0)),
            pl.BlockSpec((3, 512, 128), lambda i: (i, 0, 0)),
        ],
        out_specs=pl.BlockSpec((512, 384), lambda i: (0, i)),
        compiler_params=pltpu.CompilerParams(vmem_limit_bytes=32 * 2**20),
        name="rotate",
    )(matrix, fields)


def local(orbitals, potential, subspace):
    pairs = orbitals.reshape(2, SIDE * FLAT, 128).transpose(1, 0, 2)
    fields, matrix = sweep(
        pairs.reshape(SIDE, 2 * FLAT, 128),
        potential.reshape(SIDE, FLAT, 128),
        subspace.reshape(2, 4, 128).transpose(1, 0, 2),
    )
    return rotate(matrix.reshape(4, 512, 128), fields.reshape(BLOCKS, 512, 128))


def solution(mesh):
    placed = (P(("orb", "grid"), None), P(), P(("orb", "grid"), None))
    return jax.shard_map(
        local, mesh=mesh, in_specs=placed, out_specs=P(None, ("orb", "grid")), check_vma=False
    )
```

```python
import functools

import jax
import jax.numpy as jnp
from jax import lax
from jax.experimental import pallas as pl
from jax.experimental.pallas import tpu as pltpu
from jax.sharding import PartitionSpec as P

SIDE = 96
DEG = 6
DEVICES = 256
BLOCKS = 27
FLAT = 72
PERIOD = SIDE + 1
STEPS = PERIOD + 3 * DEG + 1
READY = 3 * DEG + 1
GROUPS = 4
MESH = pl.DeviceIdType.MESH

TOP = 12.0
CUT = 0.0
LOW = -0.25
HALF = (TOP - CUT) / 2.0
CENTRE = (TOP + CUT) / 2.0


def last_scale():
    at = (LOW - CENTRE) / HALF
    older, current = 1.0, at
    for _ in range(DEG - 1):
        older, current = current, 2.0 * at * current - older
    return 1.0 / current


def torus_peer(orb, grid, step):
    z = orb * 2 + lax.rem(grid // 2, 2)
    z = lax.rem(z + step // 32, 8)
    y = lax.rem(grid // 16 + lax.rem(step // 8, 4), 4)
    x = lax.rem(lax.rem(grid // 4, 4) + lax.rem(step // 2, 4), 4)
    core = lax.rem(grid + lax.rem(step, 2), 2)
    return z // 2, y * 16 + x * 4 + lax.rem(z, 2) * 2 + core


def sweep_kernel(
    orbitals_hbm, potential_hbm, subspace, landed, matrix,
    orbitals, potential, ring0, ring1, ring2, ring3, ring4, ring5, wells, raw, packed, staged,
    send_sem, recv_sem, near_send, near_recv, far_send, far_recv, orbitals_sem, potential_sem,
    column_sem,
):
    ring = (ring0, ring1, ring2, ring3, ring4, ring5)
    orb, grid = lax.axis_index("orb"), lax.axis_index("grid")
    me = orb * 64 + grid
    column = grid // 4 * 2 + lax.rem(grid, 2)
    depth = orb * 2 + lax.rem(grid // 2, 2)
    slot_of_me = column * 8 + depth
    downward = lax.rem(grid, 2)
    barrier = pltpu.get_barrier_semaphore()
    fetches = (
        pltpu.make_async_copy(orbitals_hbm, orbitals, orbitals_sem),
        pltpu.make_async_copy(potential_hbm, potential, potential_sem),
    )
    for fetch in fetches:
        fetch.start()

    def greet(step, carry):
        peer = torus_peer(orb, grid, step)
        pl.semaphore_signal(barrier, inc=1, device_id=peer, device_id_type=MESH)
        return carry

    lax.fori_loop(1, 32, greet, 0)
    lax.fori_loop(1, 8, lambda step, carry: greet(32 * step, carry), 0)

    lane = lax.broadcasted_iota(jnp.int32, (8, 128), 1)
    inside = lane < SIDE
    ones = jnp.where(inside, 1.0, 0.0).astype(jnp.float32)
    zeros = jnp.zeros((8, 128), jnp.float32)

    def clear(at, carry):
        for held in ring:
            for own in range(2):
                for group in range(GROUPS):
                    held[at, own, group, pl.ds(0, 8), :] = zeros
                    held[at, own, group, pl.ds(32, 8), :] = zeros
        return carry

    lax.fori_loop(0, 4, clear, 0)
    for fetch in fetches:
        fetch.wait()
    pl.semaphore_wait(barrier, 38)

    def confirm(step, carry):
        peer = torus_peer(orb, grid, step)
        pl.semaphore_signal(column_sem, inc=1, device_id=peer, device_id_type=MESH)
        return carry

    lax.fori_loop(1, 32, confirm, 0)

    own_plane = me * 3 // 8 // 3 * 3
    ordered = jnp.where(downward == 1, SIDE - 3 - own_plane, own_plane)
    near_half = lax.rem(grid // 2, 2)
    quarters = jnp.where(downward == 1, 2 - 2 * near_half, 1 + 2 * near_half)
    shift = 24 * quarters + 12 * lax.rem(grid // 4, 2)
    base = lax.rem(ordered + shift, SIDE) - DEG + PERIOD

    def position(number):
        return lax.rem(base + number, PERIOD)

    def plane_of(place):
        return jnp.where(downward == 1, SIDE - 1 - place, place)

    def to_lines(rows):
        first, second, third = rows
        return (
            jnp.where(inside, first, 0.0),
            jnp.where(inside, pltpu.roll(jnp.where(lane >= 96, first, second), 32, 1), 0.0),
            jnp.where(inside, pltpu.roll(jnp.where(lane >= 64, second, third), 64, 1), 0.0),
            jnp.where(inside, pltpu.roll(third, 96, 1), 0.0),
        )

    def to_rows(lines):
        early = pltpu.roll(lines[1], 96, 1)
        middle = pltpu.roll(lines[2], 64, 1)
        late = pltpu.roll(lines[3], 32, 1)
        return (
            jnp.where(lane < 96, lines[0], early),
            jnp.where(lane < 64, early, middle),
            jnp.where(lane < 32, middle, late),
        )

    def keep(stage, slot, own, part, values):
        rows = pl.ds(8 + 8 * part, 8)
        for group, value in enumerate(values):
            ring[stage][slot, own, group, rows, :] = value

    def zero_plane(stage, number):
        slot = lax.rem(number + 64, 4)
        place = position(number)

        @pl.when(place == SIDE)
        def _():
            for own in range(2):
                for part in range(3):
                    keep(stage, slot, own, part, [zeros] * 4)

    def take(time):
        place = position(time)
        slot = lax.rem(time, 4)
        well = lax.rem(time, 16)
        plane = plane_of(jnp.minimum(place, SIDE - 1))
        raw[...] = orbitals[plane].astype(jnp.float32)
        for part in range(3):
            rows = [potential[plane, pl.ds(24 * part + j, 8, stride=3), :] for j in range(3)]
            for group, line in enumerate(to_lines(rows)):
                wells[well, group, pl.ds(8 * part, 8), :] = 3.0 * line + 6.0
            for own in range(2):
                rows = [raw[pl.ds(48 * part + 2 * j + own, 8, stride=6), :] for j in range(3)]
                keep(0, slot, own, part, to_lines(rows))

    def advance(stage, number, own, part):
        def read(plane):
            at = lax.rem(plane + 64, 4)
            rows = [
                ring[stage - 1][at, own, group, pl.ds(8 + 8 * part, 8), :] for group in range(4)
            ]
            before = ring[stage - 1][at, own, 3, pl.ds(7 + 8 * part, 8), :]
            after = ring[stage - 1][at, own, 0, pl.ds(9 + 8 * part, 8), :]
            return [before] + rows + [after]

        behind, here, ahead = read(number - 1), read(number), read(number + 1)
        across = [u + v for u, v in zip(behind, ahead)]
        if stage == 1:
            factor = 0.5 * ones
        elif stage == DEG:
            factor = (last_scale() / 81.0) * ones
        elif stage % 2:
            factor = ones
        else:
            factor = (1.0 / 81.0) * ones
        made = []
        for group in range(4):
            centre = here[group + 1]
            both = across[group + 1] + (here[group] + here[group + 2])
            wide = both + (centre + centre)
            along = pltpu.roll(wide, 1, 1) + pltpu.roll(wide, 127, 1)
            total = (both + both) + (across[group] + across[group + 2]) + along
            well = wells[lax.rem(number + 64, 16), group, pl.ds(8 * part, 8), :]
            value = (total - well * centre) * factor
            if stage > 1:
                older = ring[stage - 2][
                    lax.rem(number + 64, 4), own, group, pl.ds(8 + 8 * part, 8), :
                ]
                value = value - (older * last_scale() if stage == DEG else older)
            made.append(value)
        return made

    def pack(time):
        place = position(time - 2 * DEG - 1)

        @pl.when(jnp.logical_and(time >= READY, place < SIDE))
        def _():
            plane = plane_of(place)
            pairs = packed[...].astype(jnp.bfloat16).reshape(FLAT, 2, 128)
            staged[pl.ds(FLAT * plane, FLAT)] = pairs
            low = (8 * plane + 2 * downward) // 3
            high = (8 * (plane + 1) + 2 * downward) // 3

            def send(target, carry):
                @pl.when(target == me)
                def _():
                    pltpu.make_async_copy(
                        staged.at[pl.ds(BLOCKS * target, BLOCKS)], landed.at[:, slot_of_me], recv_sem
                    ).start()

                @pl.when(target != me)
                def _():
                    pltpu.make_async_remote_copy(
                        staged.at[pl.ds(BLOCKS * target, BLOCKS)], landed.at[:, slot_of_me],
                        send_sem, recv_sem,
                        device_id=(target // 64, lax.rem(target, 64)), device_id_type=MESH,
                    ).start()

                return carry

            lax.fori_loop(low, high, send, 0)

    def stages(deepest, time):
        for stage in range(deepest, 0, -1):
            number = time - 2 * stage
            slot = lax.rem(number + 64, 4)
            for own in range(2):
                for part in range(3):
                    keep(stage, slot, own, part, advance(stage, number, own, part))
        take(time)
        for stage in range(deepest + 1):
            zero_plane(stage, time - 2 * stage)

    def warm(deepest, time, carry):
        stages(deepest, time)
        return carry

    def step(time, carry):
        @pl.when(time == READY - 1)
        def _():
            pl.semaphore_wait(column_sem, 31)
            pltpu.make_async_copy(subspace, matrix.at[:, column, depth], near_recv).start()

            def send(offset, inner):
                peer = torus_peer(orb, grid, offset * 32)
                pltpu.make_async_remote_copy(
                    subspace, matrix.at[:, column, depth], near_send, near_recv,
                    device_id=peer, device_id_type=MESH,
                ).start()
                return inner

            lax.fori_loop(1, 8, send, 0)

        @pl.when(time == 50)
        def _():
            group = matrix.at[:, column]
            pltpu.make_async_copy(group, group, near_recv).wait()

            def send(offset, inner):
                peer = torus_peer(orb, grid, offset)
                pltpu.make_async_remote_copy(
                    matrix.at[:, column], matrix.at[:, column], far_send, far_recv,
                    device_id=peer, device_id_type=MESH,
                ).start()
                return inner

            lax.fori_loop(1, 32, send, 0)

        pack(time)
        for own in range(2):
            for part in range(3):
                rows = to_rows(advance(DEG, time - 2 * DEG, own, part))
                for j in range(3):
                    packed[pl.ds(48 * part + 2 * j + own, 8, stride=6), :] = rows[j]
        stages(DEG - 1, time)
        return carry

    for deepest in (1, 3, 5):
        start = 3 * deepest - 3
        lax.fori_loop(start, start + 6, functools.partial(warm, deepest), 0)
    lax.fori_loop(3 * DEG, STEPS, step, 0)

    near = matrix.at[:, 0, pl.ds(0, 7)]
    pltpu.make_async_copy(near, near, near_send).wait()
    far = matrix.at[:, pl.ds(0, 31)]
    pltpu.make_async_copy(far, far, far_recv).wait()
    pltpu.make_async_copy(far, far, far_send).wait()
    pltpu.make_async_copy(landed, landed, recv_sem).wait()
    sent = staged.at[pl.ds(0, BLOCKS * (DEVICES - 1))]
    pltpu.make_async_copy(sent, sent, send_sem).wait()


def sweep(orbitals, potential, subspace):
    vmem = pl.BlockSpec(memory_space=pltpu.VMEM)
    hbm = pl.BlockSpec(memory_space=pltpu.HBM)
    return pl.pallas_call(
        sweep_kernel,
        out_shape=(
            jax.ShapeDtypeStruct((BLOCKS, DEVICES, 2, 128), jnp.bfloat16),
            jax.ShapeDtypeStruct((4, 32, 8, 2, 128), jnp.bfloat16),
        ),
        in_specs=[hbm, hbm, vmem],
        out_specs=(vmem, vmem),
        scratch_shapes=[
            pltpu.VMEM((SIDE, 2 * FLAT, 128), jnp.bfloat16),
            pltpu.VMEM((SIDE, FLAT, 128), jnp.float32),
        ] + [pltpu.VMEM((4, 2, GROUPS, 40, 128), jnp.float32)] * DEG + [
            pltpu.VMEM((16, 4, 24, 128), jnp.float32),
            pltpu.VMEM((2 * FLAT, 128), jnp.float32),
            pltpu.VMEM((2 * FLAT, 128), jnp.float32),
            pltpu.VMEM((SIDE * FLAT, 2, 128), jnp.bfloat16),
        ] + [pltpu.SemaphoreType.DMA] * 8 + [pltpu.SemaphoreType.REGULAR],
        compiler_params=pltpu.CompilerParams(
            collective_id=0, has_side_effects=True, vmem_limit_bytes=56 * 2**20
        ),
        name="sweep",
    )(orbitals, potential, subspace)


def rotate_kernel(matrix, fields, rotated, turned):
    @pl.when(pl.program_id(0) == 0)
    def _():
        for i in range(4):
            turned[pl.ds(128 * i, 128), :] = matrix[i].T

    wide = jnp.concatenate([fields[i] for i in range(3)], axis=1)
    rotated[...] = jnp.dot(
        turned[...], wide, preferred_element_type=jnp.float32
    ).astype(jnp.bfloat16)


def rotate(matrix, fields):
    return pl.pallas_call(
        rotate_kernel,
        grid=(BLOCKS // 3,),
        out_shape=jax.ShapeDtypeStruct((512, BLOCKS * 128), jnp.bfloat16),
        in_specs=[
            pl.BlockSpec((4, 512, 128), lambda i: (0, 0, 0)),
            pl.BlockSpec((3, 512, 128), lambda i: (i, 0, 0)),
        ],
        out_specs=pl.BlockSpec((512, 384), lambda i: (0, i)),
        scratch_shapes=[pltpu.VMEM((512, 512), jnp.bfloat16)],
        compiler_params=pltpu.CompilerParams(vmem_limit_bytes=58 * 2**20),
        name="rotate",
    )(matrix, fields)


def local(orbitals, potential, subspace):
    pairs = orbitals.reshape(2, SIDE * FLAT, 128).transpose(1, 0, 2)
    fields, matrix = sweep(
        pairs.reshape(SIDE, 2 * FLAT, 128),
        potential.reshape(SIDE, FLAT, 128),
        subspace.reshape(2, 4, 128).transpose(1, 0, 2),
    )
    return rotate(matrix.reshape(4, 512, 128), fields.reshape(BLOCKS, 512, 128))


def solution(mesh):
    placed = (P(("orb", "grid"), None), P(), P(("orb", "grid"), None))
    return jax.shard_map(
        local, mesh=mesh, in_specs=placed, out_specs=P(None, ("orb", "grid")), check_vma=False
    )
```

```python
import functools

import jax
import jax.numpy as jnp
from jax import lax
from jax.experimental import pallas as pl
from jax.experimental.pallas import tpu as pltpu
from jax.sharding import PartitionSpec as P

SIDE = 96
DEG = 6
DEVICES = 256
BLOCKS = 27
FLAT = 72
PERIOD = SIDE + 1
STEPS = PERIOD + 3 * DEG + 1
READY = 3 * DEG + 1
GROUPS = 4
MESH = pl.DeviceIdType.MESH

TOP = 12.0
CUT = 0.0
LOW = -0.25
HALF = (TOP - CUT) / 2.0
CENTRE = (TOP + CUT) / 2.0


def last_scale():
    at = (LOW - CENTRE) / HALF
    older, current = 1.0, at
    for _ in range(DEG - 1):
        older, current = current, 2.0 * at * current - older
    return 1.0 / current


def torus_peer(orb, grid, step):
    z = orb * 2 + lax.rem(grid // 2, 2)
    z = lax.rem(z + step // 32, 8)
    y = lax.rem(grid // 16 + lax.rem(step // 8, 4), 4)
    x = lax.rem(lax.rem(grid // 4, 4) + lax.rem(step // 2, 4), 4)
    core = lax.rem(grid + lax.rem(step, 2), 2)
    return z // 2, y * 16 + x * 4 + lax.rem(z, 2) * 2 + core


def sweep_kernel(
    orbitals_hbm, potential_hbm, subspace, landed, matrix,
    orbitals, potential, ring0, ring1, ring2, ring3, ring4, ring5, wells, raw, packed, staged,
    send_sem, recv_sem, near_send, near_recv, far_send, far_recv, orbitals_sem, potential_sem,
    column_sem,
):
    ring = (ring0, ring1, ring2, ring3, ring4, ring5)
    orb, grid = lax.axis_index("orb"), lax.axis_index("grid")
    me = orb * 64 + grid
    column = grid // 4 * 2 + lax.rem(grid, 2)
    depth = orb * 2 + lax.rem(grid // 2, 2)
    slot_of_me = column * 8 + depth
    downward = lax.rem(grid, 2)
    barrier = pltpu.get_barrier_semaphore()
    fetches = (
        pltpu.make_async_copy(orbitals_hbm, orbitals, orbitals_sem),
        pltpu.make_async_copy(potential_hbm, potential, potential_sem),
    )
    for fetch in fetches:
        fetch.start()

    def greet(step, carry):
        peer = torus_peer(orb, grid, step)
        pl.semaphore_signal(barrier, inc=1, device_id=peer, device_id_type=MESH)
        return carry

    lax.fori_loop(1, 32, greet, 0)
    lax.fori_loop(1, 8, lambda step, carry: greet(32 * step, carry), 0)

    lane = lax.broadcasted_iota(jnp.int32, (8, 128), 1)
    inside = lane < SIDE
    ones = jnp.where(inside, 1.0, 0.0).astype(jnp.float32)
    zeros = jnp.zeros((8, 128), jnp.float32)

    def clear(at, carry):
        for held in ring:
            for own in range(2):
                for group in range(GROUPS):
                    held[at, own, group, pl.ds(0, 8), :] = zeros
                    held[at, own, group, pl.ds(32, 8), :] = zeros
        return carry

    lax.fori_loop(0, 4, clear, 0)
    for fetch in fetches:
        fetch.wait()
    pl.semaphore_wait(barrier, 38)

    def confirm(step, carry):
        peer = torus_peer(orb, grid, step)
        pl.semaphore_signal(column_sem, inc=1, device_id=peer, device_id_type=MESH)
        return carry

    lax.fori_loop(1, 32, confirm, 0)

    own_plane = me * 3 // 8 // 3 * 3
    ordered = jnp.where(downward == 1, SIDE - 3 - own_plane, own_plane)
    near_half = lax.rem(grid // 2, 2)
    quarters = jnp.where(downward == 1, 2 - 2 * near_half, 1 + 2 * near_half)
    shift = 24 * quarters + 12 * lax.rem(grid // 4, 2)
    base = lax.rem(ordered + shift, SIDE) - DEG + PERIOD

    def position(number):
        return lax.rem(base + number, PERIOD)

    def plane_of(place):
        return jnp.where(downward == 1, SIDE - 1 - place, place)

    def to_lines(rows):
        first, second, third = rows
        return (
            jnp.where(inside, first, 0.0),
            jnp.where(inside, pltpu.roll(jnp.where(lane >= 96, first, second), 32, 1), 0.0),
            jnp.where(inside, pltpu.roll(jnp.where(lane >= 64, second, third), 64, 1), 0.0),
            jnp.where(inside, pltpu.roll(third, 96, 1), 0.0),
        )

    def to_rows(lines):
        early = pltpu.roll(lines[1], 96, 1)
        middle = pltpu.roll(lines[2], 64, 1)
        late = pltpu.roll(lines[3], 32, 1)
        return (
            jnp.where(lane < 96, lines[0], early),
            jnp.where(lane < 64, early, middle),
            jnp.where(lane < 32, middle, late),
        )

    def keep(stage, slot, own, part, values):
        rows = pl.ds(8 + 8 * part, 8)
        for group, value in enumerate(values):
            ring[stage][slot, own, group, rows, :] = value

    def zero_plane(stage, number):
        slot = lax.rem(number + 64, 4)
        place = position(number)

        @pl.when(place == SIDE)
        def _():
            for own in range(2):
                for part in range(3):
                    keep(stage, slot, own, part, [zeros] * 4)

    def take(time):
        place = position(time)
        slot = lax.rem(time, 4)
        well = lax.rem(time, 16)
        plane = plane_of(jnp.minimum(place, SIDE - 1))
        raw[...] = orbitals[plane].astype(jnp.float32)
        for part in range(3):
            rows = [potential[plane, pl.ds(24 * part + j, 8, stride=3), :] for j in range(3)]
            for group, line in enumerate(to_lines(rows)):
                wells[well, group, pl.ds(8 * part, 8), :] = 3.0 * line + 6.0
            for own in range(2):
                rows = [raw[pl.ds(48 * part + 2 * j + own, 8, stride=6), :] for j in range(3)]
                keep(0, slot, own, part, to_lines(rows))

    def advance(stage, number, own, part):
        def read(plane):
            at = lax.rem(plane + 64, 4)
            rows = [
                ring[stage - 1][at, own, group, pl.ds(8 + 8 * part, 8), :] for group in range(4)
            ]
            before = ring[stage - 1][at, own, 3, pl.ds(7 + 8 * part, 8), :]
            after = ring[stage - 1][at, own, 0, pl.ds(9 + 8 * part, 8), :]
            return [before] + rows + [after]

        behind, here, ahead = read(number - 1), read(number), read(number + 1)
        across = [u + v for u, v in zip(behind, ahead)]
        if stage == 1:
            factor = 0.5 * ones
        elif stage == DEG:
            factor = (last_scale() / 81.0) * ones
        elif stage % 2:
            factor = ones
        else:
            factor = (1.0 / 81.0) * ones
        made = []
        for group in range(4):
            centre = here[group + 1]
            both = across[group + 1] + (here[group] + here[group + 2])
            wide = both + (centre + centre)
            along = pltpu.roll(wide, 1, 1) + pltpu.roll(wide, 127, 1)
            total = (both + both) + (across[group] + across[group + 2]) + along
            well = wells[lax.rem(number + 64, 16), group, pl.ds(8 * part, 8), :]
            value = (total - well * centre) * factor
            if stage > 1:
                older = ring[stage - 2][
                    lax.rem(number + 64, 4), own, group, pl.ds(8 + 8 * part, 8), :
                ]
                value = value - (older * last_scale() if stage == DEG else older)
            made.append(value)
        return made

    def pack(time):
        place = position(time - 2 * DEG - 1)

        @pl.when(jnp.logical_and(time >= READY, place < SIDE))
        def _():
            plane = plane_of(place)
            pairs = packed[...].astype(jnp.bfloat16).reshape(FLAT, 2, 128)
            staged[pl.ds(FLAT * plane, FLAT)] = pairs
            low = (8 * plane + 2 * downward) // 3
            high = (8 * (plane + 1) + 2 * downward) // 3

            def send(target, carry):
                @pl.when(target == me)
                def _():
                    pltpu.make_async_copy(
                        staged.at[pl.ds(BLOCKS * target, BLOCKS)], landed.at[:, slot_of_me], recv_sem
                    ).start()

                @pl.when(target != me)
                def _():
                    pltpu.make_async_remote_copy(
                        staged.at[pl.ds(BLOCKS * target, BLOCKS)], landed.at[:, slot_of_me],
                        send_sem, recv_sem,
                        device_id=(target // 64, lax.rem(target, 64)), device_id_type=MESH,
                    ).start()

                return carry

            lax.fori_loop(low, high, send, 0)

    def stages(deepest, time):
        for stage in range(deepest, 0, -1):
            number = time - 2 * stage
            slot = lax.rem(number + 64, 4)
            for own in range(2):
                for part in range(3):
                    keep(stage, slot, own, part, advance(stage, number, own, part))
        take(time)
        for stage in range(deepest + 1):
            zero_plane(stage, time - 2 * stage)

    def warm(deepest, time, carry):
        stages(deepest, time)
        return carry

    def step(time, carry):
        @pl.when(time == READY - 1)
        def _():
            pl.semaphore_wait(column_sem, 31)
            pltpu.make_async_copy(subspace, matrix.at[:, column, depth], near_recv).start()

            def send(offset, inner):
                peer = torus_peer(orb, grid, offset * 32)
                pltpu.make_async_remote_copy(
                    subspace, matrix.at[:, column, depth], near_send, near_recv,
                    device_id=peer, device_id_type=MESH,
                ).start()
                return inner

            lax.fori_loop(1, 8, send, 0)

        @pl.when(time == 50)
        def _():
            group = matrix.at[:, column]
            pltpu.make_async_copy(group, group, near_recv).wait()

            def send(offset, inner):
                peer = torus_peer(orb, grid, offset)
                pltpu.make_async_remote_copy(
                    matrix.at[:, column], matrix.at[:, column], far_send, far_recv,
                    device_id=peer, device_id_type=MESH,
                ).start()
                return inner

            lax.fori_loop(1, 32, send, 0)

        pack(time)
        for own in range(2):
            for part in range(3):
                rows = to_rows(advance(DEG, time - 2 * DEG, own, part))
                for j in range(3):
                    packed[pl.ds(48 * part + 2 * j + own, 8, stride=6), :] = rows[j]
        stages(DEG - 1, time)
        return carry

    for deepest in (1, 3, 5):
        start = 3 * deepest - 3
        lax.fori_loop(start, start + 6, functools.partial(warm, deepest), 0)
    lax.fori_loop(3 * DEG, STEPS, step, 0)

    near = matrix.at[:, 0, pl.ds(0, 7)]
    pltpu.make_async_copy(near, near, near_send).wait()
    far = matrix.at[:, pl.ds(0, 31)]
    pltpu.make_async_copy(far, far, far_recv).wait()
    pltpu.make_async_copy(far, far, far_send).wait()
    pltpu.make_async_copy(landed, landed, recv_sem).wait()
    sent = staged.at[pl.ds(0, BLOCKS * (DEVICES - 1))]
    pltpu.make_async_copy(sent, sent, send_sem).wait()


def sweep(orbitals, potential, subspace):
    vmem = pl.BlockSpec(memory_space=pltpu.VMEM)
    hbm = pl.BlockSpec(memory_space=pltpu.HBM)
    return pl.pallas_call(
        sweep_kernel,
        out_shape=(
            jax.ShapeDtypeStruct((BLOCKS, DEVICES, 2, 128), jnp.bfloat16),
            jax.ShapeDtypeStruct((4, 32, 8, 2, 128), jnp.bfloat16),
        ),
        in_specs=[hbm, hbm, vmem],
        out_specs=(vmem, vmem),
        scratch_shapes=[
            pltpu.VMEM((SIDE, 2 * FLAT, 128), jnp.bfloat16),
            pltpu.VMEM((SIDE, FLAT, 128), jnp.float32),
        ] + [pltpu.VMEM((4, 2, GROUPS, 40, 128), jnp.float32)] * DEG + [
            pltpu.VMEM((16, 4, 24, 128), jnp.float32),
            pltpu.VMEM((2 * FLAT, 128), jnp.float32),
            pltpu.VMEM((2 * FLAT, 128), jnp.float32),
            pltpu.VMEM((SIDE * FLAT, 2, 128), jnp.bfloat16),
        ] + [pltpu.SemaphoreType.DMA] * 8 + [pltpu.SemaphoreType.REGULAR],
        compiler_params=pltpu.CompilerParams(
            collective_id=0, has_side_effects=True, vmem_limit_bytes=56 * 2**20
        ),
        name="sweep",
    )(orbitals, potential, subspace)


def rotate_kernel(matrix, fields, rotated, turned):
    @pl.when(pl.program_id(0) == 0)
    def _():
        for i in range(4):
            turned[pl.ds(128 * i, 128), :] = matrix[i].T

    wide = jnp.concatenate([fields[i] for i in range(9)], axis=1)
    rotated[...] = jnp.dot(
        turned[...], wide, preferred_element_type=jnp.float32
    ).astype(jnp.bfloat16)


def rotate(matrix, fields):
    return pl.pallas_call(
        rotate_kernel,
        grid=(BLOCKS // 9,),
        out_shape=jax.ShapeDtypeStruct((512, BLOCKS * 128), jnp.bfloat16),
        in_specs=[
            pl.BlockSpec((4, 512, 128), lambda i: (0, 0, 0)),
            pl.BlockSpec((9, 512, 128), lambda i: (i, 0, 0)),
        ],
        out_specs=pl.BlockSpec((512, 1152), lambda i: (0, i)),
        scratch_shapes=[pltpu.VMEM((512, 512), jnp.bfloat16)],
        compiler_params=pltpu.CompilerParams(vmem_limit_bytes=58 * 2**20),
        name="rotate",
    )(matrix, fields)


def local(orbitals, potential, subspace):
    pairs = orbitals.reshape(2, SIDE * FLAT, 128).transpose(1, 0, 2)
    fields, matrix = sweep(
        pairs.reshape(SIDE, 2 * FLAT, 128),
        potential.reshape(SIDE, FLAT, 128),
        subspace.reshape(2, 4, 128).transpose(1, 0, 2),
    )
    return rotate(matrix.reshape(4, 512, 128), fields.reshape(BLOCKS, 512, 128))


def solution(mesh):
    placed = (P(("orb", "grid"), None), P(), P(("orb", "grid"), None))
    return jax.shard_map(
        local, mesh=mesh, in_specs=placed, out_specs=P(None, ("orb", "grid")), check_vma=False
    )
```
